256 devices in a mesh: freq: 16 (over y_hi, z), sens: 8 (over x, y_lo), op: 2 (over core).
Axes of the slice: x: 4, y: 4 (y_hi: 2, y_lo: 2; y = y_hi * 2 + y_lo), z: 8, core: 2. Of those that a mesh axis runs over, the one named last changes fastest.
Arguments:
- tensor: bfloat16 [8, 16384, 4096], P('op', 'freq', 'sens'), may hold values from -768 to 768
- b_start: bfloat16 [4096, 256], P(('sens', 'freq', 'op')), may hold values from -0.09375 to 0.09375
- c_factor: bfloat16 [8, 256], P('op'), may hold values from 0.5 to 1.5
Outputs:
- a_factor: float32 [16384, 256], P(('freq', 'sens', 'op'))
- b_factor: float32 [4096, 256], P(('sens', 'freq', 'op'))
The draws below stay inside these ranges and needn't reach their ends.
All inputs are finite; a program needn't handle non-finite values.
Results may differ from the reference program's by a relative error of at most 0.0031.
Values may be sent and summed in bfloat16 or wider, within the bound.
No kernel may reach another device: no remote copies, remote signals or barrier semaphores. Data moves between devices by JAX's collectives and lax.ppermute only.
A program may use at most 64 MiB of HBM per device.

```python
import jax
import jax.numpy as jnp
from jax import lax

RANK = 256
FREQS = 16384
PAIRS = 4096
POINTS = 8


def level_of(key, extent, cuts, low, largest):
    loudness = 1.0
    for dim, blocks in cuts:
        steps = jax.random.uniform(jax.random.fold_in(jax.random.fold_in(key, 6), dim), (blocks,), jnp.float32, low / len(cuts), largest / len(cuts))
        loudness = loudness * jnp.repeat(jnp.exp(steps), extent[dim] // blocks).reshape((-1,) + (1,) * (len(extent) - 1 - dim))
    return loudness


def scatter_about(own_key, dims, width, bound, shards=(), held_as=jnp.bfloat16):
    gain = level_of(own_key, dims, shards, -0.22, 0.18) if shards else 1.0
    array = jax.random.normal(own_key, dims, jnp.float32) * width * gain
    return jnp.minimum(jnp.maximum(array, -bound), bound).astype(held_as)


def setup_inputs(seed: int = 0) -> dict:
    keys = jax.random.split(jax.random.key(seed), 4)
    return {
        "tensor": scatter_about(keys[0], (POINTS, FREQS, PAIRS), 128.0, 768.0, ((0, 2), (1, 16), (2, 8))),
        "b_start": scatter_about(keys[1], (PAIRS, RANK), PAIRS ** -0.5, 0.09375, ((0, 256),)),
        "c_factor": jnp.clip(0.5 + 1.0 * jax.random.uniform(keys[2], (POINTS, RANK), jnp.float32) ** level_of(keys[2], (POINTS, RANK), ((0, 2),), -0.2, 0.2), 0.5, 1.5).astype(jnp.bfloat16),
    }


EPS = 1e-06

def solve_rows(right_rows, gram):
    factor = jnp.linalg.cholesky(gram)
    lower_sol = jax.scipy.linalg.solve_triangular(factor, right_rows.T, lower=True)
    return jax.scipy.linalg.solve_triangular(factor, lower_sol, lower=True, trans=1).T

def reference(tensor, b_start, c_factor):
    b_gram = jnp.dot(b_start.T.astype(jnp.float32), b_start.astype(jnp.float32), preferred_element_type=jnp.float32)
    c_gram = jnp.dot(c_factor.T.astype(jnp.float32), c_factor.astype(jnp.float32), preferred_element_type=jnp.float32)
    c_float = c_factor.astype(jnp.float32)
    b_float = b_start.astype(jnp.float32)
    first_product = jnp.zeros((FREQS, RANK), jnp.float32)
    for point in range(POINTS):
        weights = (b_float * c_float[point][None, :]).astype(jnp.bfloat16)
        first_product = first_product + jnp.dot(tensor[point].astype(jnp.float32), weights.astype(jnp.float32), preferred_element_type=jnp.float32)
    a_raw = solve_rows(first_product, b_gram * c_gram)
    column_scale = jnp.sqrt(lax.optimization_barrier(jnp.sum(a_raw * a_raw, axis=0)) / FREQS + EPS)
    a_factor = a_raw / column_scale[None, :]
    a_gram = jnp.dot(a_factor.T.astype(jnp.float32), a_factor.astype(jnp.float32), precision=lax.Precision.HIGHEST, preferred_element_type=jnp.float32)
    a_rows = a_factor.astype(jnp.bfloat16)
    a_float = a_rows.astype(jnp.float32)
    second_product = jnp.zeros((PAIRS, RANK), jnp.float32)
    for point in range(POINTS):
        weights = (a_float * c_float[point][None, :]).astype(jnp.bfloat16)
        second_product = second_product + jnp.dot(tensor[point].T.astype(jnp.float32), weights.astype(jnp.float32), preferred_element_type=jnp.float32)
    b_factor = solve_rows(second_product, a_gram * c_gram)
    return (a_factor, b_factor)
```

```python
import functools

import jax
import jax.numpy as jnp
from jax import lax
from jax.experimental import pallas as pl
from jax.experimental.pallas import tpu as pltpu
from jax.sharding import PartitionSpec as P

EPS = 1e-06
F32 = jnp.float32
BF16 = jnp.bfloat16
HIGH = lax.Precision.HIGHEST
WHOLE = pl.BlockSpec(memory_space=pltpu.VMEM)


def tree_sum(terms):
    while len(terms) > 1:
        pairs = [terms[i] + terms[i + 1] for i in range(0, len(terms) - 1, 2)]
        terms = pairs + terms[len(terms) - len(terms) % 2 :]
    return terms[0]


def sweep(ref):
    tile = (8, 128)
    lane = lax.broadcasted_iota(jnp.int32, tile, 1)
    sub = lax.broadcasted_iota(jnp.int32, tile, 0)

    def step(k, carry):
        row = ref[k]
        from_block = lane - k * 8
        in_block = (from_block >= 0) & (from_block < 8)

        def column(block, j):
            return jnp.take_along_axis(block, jnp.full(tile, k * 8 + j, jnp.int32), axis=1)

        columns = [column(row, j) for j in range(8)]
        d = {}
        for i in range(8):
            for j in range(i + 1):
                d[i, j] = jnp.broadcast_to(columns[j][i : i + 1, :], tile)

        def entry(i, j):
            return d[max(i, j), min(i, j)]

        for p in range(8):
            inverse = 1.0 / d[p, p]
            pivots = [entry(i, p) for i in range(8)]
            scaled = [pivots[i] * inverse for i in range(8)]
            for i in range(8):
                for j in range(i + 1):
                    if i != p and j != p:
                        d[i, j] = d[i, j] - scaled[i] * pivots[j]
            for i in range(8):
                if i != p:
                    d[max(i, p), min(i, p)] = scaled[i]
            d[p, p] = -inverse
        source = jnp.where(in_block, jnp.where(from_block == sub, 1.0, 0.0), -row)
        sources = [jnp.broadcast_to(source[j : j + 1, :], tile) for j in range(8)]
        rows = [tree_sum([entry(i, j) * sources[j] for j in range(8)]) for i in range(8)]
        new_row = rows[0]
        for i in range(1, 8):
            new_row = jnp.where(sub == i, rows[i], new_row)
        for b in range(16):
            block = ref[b]
            change = tree_sum([column(block, j) * rows[j] for j in range(8)])
            ref[b] = jnp.where(in_block, 0.0, block) - change
        ref[k] = new_row
        return carry

    lax.fori_loop(0, 16, step, 0)


def dot(a, b):
    return jnp.dot(a, b, precision=HIGH, preferred_element_type=F32)


def dot_tn(a, b):
    return lax.dot_general(a, b, (((0,), (0,)), ((), ())), precision=HIGH, preferred_element_type=F32)


def dot_nt(a, b):
    return lax.dot_general(a, b, (((1,), (1,)), ((), ())), precision=HIGH, preferred_element_type=F32)


def invert(gram, inverse_ref, block_ref):
    g12 = gram[0:128, 128:256]
    block_ref[...] = gram[0:128, 0:128].reshape(16, 8, 128)
    sweep(block_ref)
    x = -block_ref[...].reshape(128, 128)
    b = dot(x, g12)
    block_ref[...] = (gram[128:256, 128:256] - dot_tn(g12, b)).reshape(16, 8, 128)
    sweep(block_ref)
    y = -block_ref[...].reshape(128, 128)
    z12 = -dot(b, y)
    inverse_ref[0:128, 0:128] = x - dot_nt(z12, b)
    inverse_ref[0:128, 128:256] = z12
    inverse_ref[128:256, 0:128] = z12.T
    inverse_ref[128:256, 128:256] = y


def gram_inverse_kernel(mine_ref, other_ref, c_ref, out_ref, block_ref):
    gram = (mine_ref[...] + other_ref[...]) * dot_tn(c_ref[...], c_ref[...])
    invert(gram, out_ref, block_ref)


def gram_inverse(mine, other, c_all):
    return pl.pallas_call(
        gram_inverse_kernel,
        out_shape=jax.ShapeDtypeStruct(mine.shape, F32),
        in_specs=[WHOLE] * 3,
        out_specs=WHOLE,
        scratch_shapes=[pltpu.VMEM((16, 8, 128), F32)],
        cost_estimate=pl.CostEstimate(flops=10**10, bytes_accessed=10**6, transcendentals=0),
        name="gram_inverse",
    )(mine, other, c_all)


def finish_kernel(total, parts_ref, second_ref, raw_ref, c_ref, a_ref, b_ref, inverse_ref, block_ref):
    parts = parts_ref[...]
    size = parts.shape[-1]
    squares = jnp.sum(jnp.sum(parts[:, 16:24, :], axis=0), axis=0, keepdims=True)
    scale = jnp.sqrt(squares / total + EPS)
    a_ref[...] = raw_ref[...] / scale
    first = lax.broadcasted_iota(jnp.int32, (8, size), 0) == 0
    inverse_scale = jnp.where(first, 1.0 / scale, 0.0)
    gram = parts[:, 0:16, :].reshape(size, size) * dot_tn(inverse_scale, inverse_scale)
    gram = gram * dot_tn(c_ref[...], c_ref[...])
    invert(gram, inverse_ref, block_ref)
    b_ref[...] = dot(second_ref[...] / scale, inverse_ref[...])


def finish(parts, second, raw, c_all, total):
    size = raw.shape[1]
    return pl.pallas_call(
        functools.partial(finish_kernel, float(total)),
        out_shape=(jax.ShapeDtypeStruct(raw.shape, F32), jax.ShapeDtypeStruct(second.shape, F32)),
        in_specs=[WHOLE] * 4,
        out_specs=(WHOLE, WHOLE),
        scratch_shapes=[pltpu.VMEM((size, size), F32), pltpu.VMEM((16, 8, 128), F32)],
        cost_estimate=pl.CostEstimate(flops=10**10, bytes_accessed=10**6, transcendentals=0),
        name="finish",
    )(parts, second, raw, c_all)


def exchange(block, axes):
    return lax.all_to_all(block, axes, 0, 0, tiled=True)


def spread(block, axes):
    count = lax.axis_size(axes)
    return exchange(jnp.broadcast_to(block[None], (count,) + block.shape), axes)


def swap(block):
    return lax.ppermute(block, "op", [(0, 1), (1, 0)])


def add_cores(partial):
    core = lax.axis_index("op")
    keep = lax.dynamic_index_in_dim(partial, core, 1, keepdims=False)
    send = lax.dynamic_index_in_dim(partial, 1 - core, 1, keepdims=False)
    return keep + swap(send)


def shards(tensor, b_start, c_factor):
    points, freq_count, pair_count = tensor.shape
    rank = b_start.shape[1]
    freqs, senses = lax.axis_size("freq"), lax.axis_size("sens")
    core, sens = lax.axis_index("op"), lax.axis_index("sens")
    total_freqs = freq_count * freqs
    c_float = c_factor.astype(F32)
    c_all = lax.all_gather(c_factor, "op", axis=0, tiled=True).astype(F32)

    b_local = spread(b_start, ("freq", "op")).reshape(pair_count, rank)
    half = lax.dynamic_slice_in_dim(b_local, core * (pair_count // 2), pair_count // 2, 0)
    b_half = spread(half, "sens").reshape(senses * (pair_count // 2), rank)
    b_mine = lax.dot_general(b_half, b_half, (((0,), (0,)), ((), ())), preferred_element_type=F32)
    inverse_one = gram_inverse(b_mine, swap(b_mine), c_all)

    weights_one = (b_local.astype(F32)[None] * c_float[:, None, :]).astype(BF16)
    part_one = jnp.einsum("kij,kjr->ir", tensor, weights_one, preferred_element_type=F32)
    own = freq_count // (2 * senses)
    owned = add_cores(part_one.reshape(senses, 2, own, rank))
    first = jnp.sum(exchange(owned, "sens"), axis=0)
    a_raw = jnp.dot(first, inverse_one, precision=HIGH, preferred_element_type=F32)

    a_pair = lax.all_gather(a_raw.astype(BF16), "op", axis=0, tiled=True)
    a_rows = spread(a_pair, "sens").reshape(freq_count, rank)
    weights_two = (a_rows.astype(F32)[None] * c_float[:, None, :]).astype(BF16)
    part_two = jnp.einsum("kij,kir->jr", tensor, weights_two, preferred_element_type=F32)
    own_pairs = pair_count // (2 * freqs)
    owned_pairs = add_cores(part_two.reshape(freqs, 2, own_pairs, rank))
    a_part = lax.dot_general(a_rows, a_rows, (((0,), (0,)), ((), ())), preferred_element_type=F32)
    strip = rank // (2 * senses)
    a_strip = lax.dynamic_slice_in_dim(a_part, (sens * 2 + core) * strip, strip, 0)
    squares = jnp.sum((a_raw * a_raw).reshape(own // 8, 8, rank), axis=0)
    along = jnp.concatenate([a_strip, squares], axis=0)
    along = jnp.broadcast_to(along[None], (freqs,) + along.shape)
    summed = jnp.sum(exchange(jnp.concatenate([owned_pairs, along], axis=1), "freq"), axis=0)
    second, strips = summed[:own_pairs], summed[own_pairs:]
    strips = lax.all_gather(strips[None], "op", axis=0, tiled=True)
    parts = spread(strips, "sens").reshape(2 * senses, strip + 8, rank)
    return finish(parts, second, a_raw, c_all, total_freqs)


def solution(mesh):
    in_specs = (P("op", "freq", "sens"), P(("sens", "freq", "op"), None), P("op", None))
    out_specs = (P(("freq", "sens", "op"), None), P(("sens", "freq", "op"), None))
    return jax.shard_map(shards, mesh=mesh, in_specs=in_specs, out_specs=out_specs, check_vma=False)
```

```python
import functools

import jax
import jax.numpy as jnp
from jax import lax
from jax.experimental import pallas as pl
from jax.experimental.pallas import tpu as pltpu
from jax.sharding import PartitionSpec as P

EPS = 1e-06
F32 = jnp.float32
BF16 = jnp.bfloat16
HIGH = lax.Precision.HIGHEST
WHOLE = pl.BlockSpec(memory_space=pltpu.VMEM)
TILE = (8, 128)
PRODUCT_PARAMS = pltpu.CompilerParams(vmem_limit_bytes=51 * 2**20)
PARAMS = pltpu.CompilerParams(vmem_limit_bytes=24 * 2**20)
SCALARS = pl.BlockSpec(memory_space=pltpu.SMEM)
PRODUCT_COST = pl.CostEstimate(flops=2 * 10**9, bytes_accessed=6 * 10**6, transcendentals=0)
SOLVE_COST = pl.CostEstimate(flops=2 * 10**10, bytes_accessed=10**6, transcendentals=0)


def tree_sum(terms):
    while len(terms) > 1:
        pairs = [terms[i] + terms[i + 1] for i in range(0, len(terms) - 1, 2)]
        terms = pairs + terms[len(terms) - len(terms) % 2 :]
    return terms[0]


def column(block, lane):
    return jnp.take_along_axis(block, jnp.full(TILE, lane, jnp.int32), axis=1)


def invert_block(d):
    def entry(i, j):
        return d[max(i, j), min(i, j)]

    for p in range(0, 8, 2):
        q = p + 1
        first, cross, second = d[p, p], d[q, p], d[q, q]
        determinant = first * second - cross * cross
        guess = pl.reciprocal(determinant, approx=True)
        guess = guess * (2.0 - determinant * guess)
        guess = guess * (2.0 - determinant * guess)
        pp, qp, qq = second * guess, -(cross * guess), first * guess
        rest = [i for i in range(8) if i not in (p, q)]
        left = {i: entry(i, p) for i in rest}
        right = {i: entry(i, q) for i in rest}
        left_new = {i: left[i] * pp + right[i] * qp for i in rest}
        right_new = {i: left[i] * qp + right[i] * qq for i in rest}
        for i in rest:
            for j in rest:
                if j <= i:
                    d[i, j] = d[i, j] - (left_new[i] * left[j] + right_new[i] * right[j])
        for i in rest:
            d[max(i, p), min(i, p)] = left_new[i]
            d[max(i, q), min(i, q)] = right_new[i]
        d[p, p], d[q, p], d[q, q] = -pp, -qp, -qq
    return entry


def sweep_panel(ref, start, half, base):
    lane = lax.broadcasted_iota(jnp.int32, TILE, 1)
    sub = lax.broadcasted_iota(jnp.int32, TILE, 0)
    rows = [
        [ref[pl.ds(pl.multiple_of(start + 8 * m, 8), 8), 128 * h : 128 * h + 128] for h in range(2)]
        for m in range(4)
    ]
    for m in range(4):
        from_block = lane - (base + 8 * m)
        in_block = (from_block >= 0) & (from_block < 8)
        columns = [[column(rows[g][half], base + 8 * m + j) for j in range(8)] for g in range(4)]
        d = {
            (i, j): jnp.broadcast_to(columns[m][j][i : i + 1, :], TILE)
            for i in range(8)
            for j in range(i + 1)
        }
        entry = invert_block(d)
        new, spread_rows = [], []
        for h in range(2):
            source = -rows[m][h]
            if h == half:
                source = jnp.where(in_block, jnp.where(from_block == sub, 1.0, 0.0), source)
            sources = [jnp.broadcast_to(source[j : j + 1, :], TILE) for j in range(8)]
            spread_rows.append(
                [tree_sum([entry(i, j) * sources[j] for j in range(8)]) for i in range(8)]
            )
            row = spread_rows[h][0]
            for i in range(1, 8):
                row = jnp.where(sub == i, spread_rows[h][i], row)
            new.append(row)
        for g in range(4):
            if g == m:
                continue
            for h in range(2):
                block = rows[g][h]
                if h == half:
                    block = jnp.where(in_block, 0.0, block)
                rows[g][h] = block - tree_sum([columns[g][j] * spread_rows[h][j] for j in range(8)])
        rows[m] = new
    return jnp.concatenate([jnp.concatenate(row, axis=1) for row in rows], axis=0)


def sweep(ref):
    lane = lax.broadcasted_iota(jnp.int32, (256, 256), 1)
    for half in range(2):

        def step(k, carry):
            start = half * 128 + k * 32
            panel = pl.ds(pl.multiple_of(start, 32), 32)
            old = ref[panel, :]
            new = sweep_panel(ref, start, half, k * 32)
            in_panel = (lane >= start) & (lane < start + 32)
            ref[...] = jnp.where(in_panel, 0.0, ref[...]) - dot_tn(old, new)
            ref[panel, :] = new
            return carry

        lax.fori_loop(0, 4, step, 0)


def dot(a, b):
    return jnp.dot(a, b, precision=HIGH, preferred_element_type=F32)


def dot_tn(a, b):
    return lax.dot_general(a, b, (((0,), (0,)), ((), ())), precision=HIGH, preferred_element_type=F32)


def diagonal_of(gram):
    on_diagonal = lax.broadcasted_iota(jnp.int32, gram.shape, 0) == lax.broadcasted_iota(jnp.int32, gram.shape, 1)
    return jnp.sum(jnp.where(on_diagonal, gram, 0.0), axis=0, keepdims=True)


def diagonal_scale(gram):
    return lax.rsqrt(diagonal_of(gram))


def outer(row):
    first = lax.broadcasted_iota(jnp.int32, (8, row.shape[1]), 0) == 0
    row = jnp.where(first, row, 0.0)
    return dot_tn(row, row)


def gram_inverse_kernel(mine_ref, other_ref, c_ref, out_ref):
    gram = (mine_ref[...] + other_ref[...]) * dot_tn(c_ref[...], c_ref[...])
    scale = outer(diagonal_scale(gram))
    out_ref[...] = gram * scale
    sweep(out_ref)
    out_ref[...] = -out_ref[...] * scale


def gram_inverse(mine, other, c_all):
    return pl.pallas_call(
        gram_inverse_kernel,
        out_shape=jax.ShapeDtypeStruct(mine.shape, F32),
        in_specs=[WHOLE] * 3,
        out_specs=WHOLE,
        cost_estimate=SOLVE_COST,
        compiler_params=PARAMS,
        name="gram_inverse",
    )(mine, other, c_all)


def in_order(mine, other, core):
    first = jnp.where(core == 0, mine, other)
    second = jnp.where(core == 0, other, mine)
    return jnp.concatenate([first[:, None], second[:, None]], axis=1)


def scaled_inverse_kernel(total, core_ref, mine_ref, other_ref, raw_ref, c_ref, a_ref, inverse_ref, before_ref, after_ref):
    size = raw_ref.shape[1]
    gram = in_order(mine_ref[...], other_ref[...], core_ref[0]).reshape(size, size)
    squares = diagonal_of(gram)
    scale = jnp.sqrt(squares / total + EPS)
    a_ref[...] = raw_ref[...] / scale
    gram = gram * dot_tn(c_ref[...], c_ref[...])
    before = diagonal_scale(gram)
    inverse_ref[...] = gram * outer(before)
    sweep(inverse_ref)
    inverse_ref[...] = -inverse_ref[...]
    before_ref[...] = jnp.broadcast_to(before, before_ref.shape)
    after_ref[...] = jnp.broadcast_to(before * scale, after_ref.shape)


def scaled_inverse(core, mine, other, raw, c_all, total):
    size = raw.shape[1]
    row = jax.ShapeDtypeStruct((8, size), F32)
    return pl.pallas_call(
        functools.partial(scaled_inverse_kernel, float(total)),
        out_shape=(jax.ShapeDtypeStruct(raw.shape, F32), jax.ShapeDtypeStruct((size, size), F32), row, row),
        in_specs=[SCALARS] + [WHOLE] * 4,
        out_specs=(WHOLE,) * 4,
        cost_estimate=SOLVE_COST,
        compiler_params=PARAMS,
        name="scaled_inverse",
    )(core, mine, other, raw, c_all)


def first_product_kernel(core_ref, tensor_ref, mine_ref, other_ref, c_ref, keep_ref, send_ref, held_ref, b_ref, arrived):
    core = core_ref[0]
    points, rows, depth = tensor_ref.shape
    owners, own, rank = keep_ref.shape
    steps = arrived.shape[0]
    height = rows // steps

    def load(i):
        part = pl.ds(pl.multiple_of(i * height, height), height)
        return pltpu.make_async_copy(tensor_ref.at[:, part, :], held_ref.at[:, part, :], arrived.at[i])

    for i in range(steps):
        load(i).start()
    b_ref[...] = in_order(mine_ref[...], other_ref[...], core).reshape(b_ref.shape)
    few = owners // steps

    def step(i, carry):
        load(i).wait()
        total = None
        for k in range(points):
            block = held_ref[k, pl.ds(pl.multiple_of(i * height, height), height), :]
            term = jnp.dot(block, b_ref[...], preferred_element_type=F32) * c_ref[k : k + 1, :]
            total = term if total is None else total + term
        total = total.reshape(few, 2, own, rank)
        keep_ref[pl.ds(i * few, few)] = jnp.where(core == 0, total[:, 0], total[:, 1])
        send_ref[pl.ds(i * few, few)] = jnp.where(core == 0, total[:, 1], total[:, 0])
        return carry

    lax.fori_loop(0, steps, step, 0)


def first_product(core, tensor, mine, other, c_all, owners):
    points, rows, depth = tensor.shape
    rank = mine.shape[-1]
    part = jax.ShapeDtypeStruct((owners, rows // (2 * owners), rank), F32)
    return pl.pallas_call(
        first_product_kernel,
        out_shape=(part, part),
        in_specs=[SCALARS, pl.BlockSpec(memory_space=pl.ANY)] + [WHOLE] * 3,
        out_specs=(WHOLE,) * 2,
        scratch_shapes=[
            pltpu.VMEM(tensor.shape, BF16),
            pltpu.VMEM((depth, rank), BF16),
            pltpu.SemaphoreType.DMA((4,)),
        ],
        compiler_params=PRODUCT_PARAMS,
        cost_estimate=PRODUCT_COST,
        name="first_product",
    )(core, tensor, mine, other, c_all)


def second_product_kernel(core_ref, tensor_ref, mine_ref, other_ref, c_ref, keep_ref, send_ref, held_ref, a_ref, sum_ref, arrived):
    core = core_ref[0]
    owners, own, rank = keep_ref.shape

    def load(k):
        return pltpu.make_async_copy(tensor_ref.at[k], held_ref.at[k], arrived.at[k])

    for k in range(tensor_ref.shape[0]):
        load(k).start()
    a_rows = in_order(mine_ref[...], other_ref[...], core).reshape(a_ref.shape[1], a_ref.shape[0])
    a_ref[...] = a_rows.T
    sum_ref[...] = jnp.zeros_like(sum_ref)

    def step(k, carry):
        load(k).wait()
        term = jnp.dot(a_ref[...], held_ref[k], preferred_element_type=F32)
        sum_ref[...] += term * jnp.concatenate([c_ref[k]] * (term.shape[1] // 128), axis=1)
        return carry

    lax.fori_loop(0, tensor_ref.shape[0], step, 0)
    total = sum_ref[...].T.reshape(owners, 2, own, rank)
    keep_ref[...] = jnp.where(core == 0, total[:, 0], total[:, 1])
    send_ref[...] = jnp.where(core == 0, total[:, 1], total[:, 0])


def second_product(core, tensor, mine, other, c_columns, owners):
    points, depth, rows = tensor.shape
    rank = mine.shape[-1]
    part = jax.ShapeDtypeStruct((owners, rows // (2 * owners), rank), F32)
    return pl.pallas_call(
        second_product_kernel,
        out_shape=(part, part),
        in_specs=[SCALARS, pl.BlockSpec(memory_space=pl.ANY)] + [WHOLE] * 3,
        out_specs=(WHOLE, WHOLE),
        scratch_shapes=[
            pltpu.VMEM(tensor.shape, BF16),
            pltpu.VMEM((rank, depth), BF16),
            pltpu.VMEM((rank, rows), F32),
            pltpu.SemaphoreType.DMA((points,)),
        ],
        compiler_params=PRODUCT_PARAMS,
        cost_estimate=PRODUCT_COST,
        name="second_product",
    )(core, tensor, mine, other, c_columns)


def solve_kernel(parts_ref, inverse_ref, raw_ref, rows_ref):
    raw = dot(jnp.sum(parts_ref[...], axis=0), inverse_ref[...])
    raw_ref[...] = raw
    rows_ref[...] = jnp.broadcast_to(raw.astype(BF16)[None], rows_ref.shape)


def solve(parts, inverse, copies):
    own = parts.shape[1:]
    return pl.pallas_call(
        solve_kernel,
        out_shape=(jax.ShapeDtypeStruct(own, F32), jax.ShapeDtypeStruct((copies,) + own, BF16)),
        in_specs=[WHOLE] * 2,
        out_specs=(WHOLE,) * 2,
        compiler_params=PARAMS,
        name="solve",
    )(parts, inverse)


def sum_spread_kernel(parts_ref, out_ref):
    out_ref[...] = jnp.broadcast_to(jnp.sum(parts_ref[...], axis=0)[None], out_ref.shape)


def sum_spread(parts, copies):
    return pl.pallas_call(
        sum_spread_kernel,
        out_shape=jax.ShapeDtypeStruct((copies,) + parts.shape[1:], F32),
        in_specs=[WHOLE],
        out_specs=WHOLE,
        compiler_params=PARAMS,
        name="sum_spread",
    )(parts)


def last_rows_kernel(parts_ref, inverse_ref, before_ref, after_ref, out_ref):
    rows = jnp.sum(parts_ref[...], axis=0) * before_ref[0:1, :]
    out_ref[...] = dot(rows, inverse_ref[...]) * after_ref[0:1, :]


def last_rows(parts, inverse, before, after):
    return pl.pallas_call(
        last_rows_kernel,
        out_shape=jax.ShapeDtypeStruct(parts.shape[1:], F32),
        in_specs=[WHOLE] * 4,
        out_specs=WHOLE,
        compiler_params=PARAMS,
        name="last_rows",
    )(parts, inverse, before, after)


def gram_strips_kernel(strip_ref, mine_ref, other_ref, out_ref, gram_ref):
    gram = None
    for ref in (mine_ref, other_ref):
        rows = ref[...].reshape(-1, ref.shape[-1])
        term = lax.dot_general(rows, rows, (((0,), (0,)), ((), ())), preferred_element_type=F32)
        gram = term if gram is None else gram + term
    gram_ref[...] = gram
    height = out_ref.shape[1]
    strip = gram_ref[pl.ds(pl.multiple_of(strip_ref[0] * height, height), height), :]
    out_ref[...] = jnp.broadcast_to(strip[None], out_ref.shape)


def gram_strips(strip, mine, other, copies, strips):
    rank = mine.shape[-1]
    return pl.pallas_call(
        gram_strips_kernel,
        out_shape=jax.ShapeDtypeStruct((copies, rank // strips, rank), F32),
        in_specs=[SCALARS, WHOLE, WHOLE],
        out_specs=WHOLE,
        scratch_shapes=[pltpu.VMEM((rank, rank), F32)],
        cost_estimate=pl.CostEstimate(flops=10**9, bytes_accessed=10**6, transcendentals=0),
        compiler_params=PARAMS,
        name="gram_strips",
    )(strip, mine, other)


def add_after_kernel(keep_ref, received_ref, gate_ref, out_ref):
    out_ref[...] = keep_ref[...] + received_ref[...]


def add_after(keep, received, gate):
    return pl.pallas_call(
        add_after_kernel,
        out_shape=jax.ShapeDtypeStruct(keep.shape, F32),
        in_specs=[WHOLE, WHOLE, pl.BlockSpec(memory_space=pl.ANY)],
        out_specs=WHOLE,
        compiler_params=PARAMS,
        name="add_after",
    )(keep, received, gate)


def exchange(block, axes):
    return lax.all_to_all(block, axes, 0, 0, tiled=True)


def spread(block, axes):
    return exchange(jnp.broadcast_to(block[None], (lax.axis_size(axes),) + block.shape), axes)


def swap(block):
    return lax.ppermute(block, "op", [(0, 1), (1, 0)])


def shards(tensor, b_start, c_factor):
    points, freq_count, pair_count = tensor.shape
    rank = b_start.shape[1]
    freqs, senses = lax.axis_size("freq"), lax.axis_size("sens")
    core_id = lax.axis_index("op")
    core = core_id.astype(jnp.int32)[None]
    strip = (lax.axis_index("sens") * 2 + core_id).astype(jnp.int32)[None]
    c_float = c_factor.astype(F32)
    c_all = jnp.concatenate([c_float, swap(c_factor).astype(F32)], axis=0)
    c_columns = jnp.broadcast_to(c_float[:, :, None], (points, rank, 128))

    b_mine = spread(b_start, "freq")
    b_other = swap(b_mine)
    b_half = spread(b_mine.reshape(-1, rank), "sens").reshape(-1, rank)
    b_part = lax.dot_general(b_half, b_half, (((0,), (0,)), ((), ())), preferred_element_type=F32)
    inverse_one = gram_inverse(b_part, swap(b_part), c_all)
    keep, send = first_product(core, tensor, b_mine, b_other, c_all, senses)
    a_raw, a_spread = solve(exchange(keep + swap(send), "sens"), inverse_one, senses)

    a_mine = exchange(a_spread, "sens")
    a_other = swap(a_mine)
    strips = exchange(gram_strips(strip, a_mine, a_other, freqs, 2 * senses), "freq")
    keep, send = second_product(core, tensor, a_mine, a_other, c_columns, freqs)
    strips_mine = exchange(sum_spread(strips, senses), "sens")
    strips_other = swap(strips_mine)
    second = exchange(add_after(keep, swap(send), strips_mine), "freq")
    a_factor, inverse_two, before, after = scaled_inverse(
        core, strips_mine, strips_other, a_raw, c_all, freq_count * freqs
    )
    return a_factor, last_rows(second, inverse_two, before, after)


def solution(mesh):
    in_specs = (P("op", "freq", "sens"), P(("sens", "freq", "op"), None), P("op", None))
    out_specs = (P(("freq", "sens", "op"), None), P(("sens", "freq", "op"), None))
    return jax.shard_map(shards, mesh=mesh, in_specs=in_specs, out_specs=out_specs, check_vma=False)
```

```python
import functools

import jax
import jax.numpy as jnp
from jax import lax
from jax.experimental import pallas as pl
from jax.experimental.pallas import tpu as pltpu
from jax.sharding import PartitionSpec as P

EPS = 1e-06
F32 = jnp.float32
BF16 = jnp.bfloat16
HIGH = lax.Precision.HIGHEST
WHOLE = pl.BlockSpec(memory_space=pltpu.VMEM)
TILE = (8, 128)
PRODUCT_PARAMS = pltpu.CompilerParams(vmem_limit_bytes=51 * 2**20)
PARAMS = pltpu.CompilerParams(vmem_limit_bytes=24 * 2**20)
SCALARS = pl.BlockSpec(memory_space=pltpu.SMEM)
PRODUCT_COST = pl.CostEstimate(flops=2 * 10**9, bytes_accessed=6 * 10**6, transcendentals=0)
SOLVE_COST = pl.CostEstimate(flops=2 * 10**10, bytes_accessed=10**6, transcendentals=0)


def tree_sum(terms):
    while len(terms) > 1:
        pairs = [terms[i] + terms[i + 1] for i in range(0, len(terms) - 1, 2)]
        terms = pairs + terms[len(terms) - len(terms) % 2 :]
    return terms[0]


def column(block, lane):
    return jnp.take_along_axis(block, jnp.full(TILE, lane, jnp.int32), axis=1)


def invert_block(d):
    def entry(i, j):
        return d[max(i, j), min(i, j)]

    for p in range(0, 8, 2):
        q = p + 1
        first, cross, second = d[p, p], d[q, p], d[q, q]
        determinant = first * second - cross * cross
        guess = pl.reciprocal(determinant, approx=True)
        guess = guess * (2.0 - determinant * guess)
        pp, qp, qq = second * guess, -(cross * guess), first * guess
        rest = [i for i in range(8) if i not in (p, q)]
        left = {i: entry(i, p) for i in rest}
        right = {i: entry(i, q) for i in rest}
        left_new = {i: left[i] * pp + right[i] * qp for i in rest}
        right_new = {i: left[i] * qp + right[i] * qq for i in rest}
        for i in rest:
            for j in rest:
                if j <= i:
                    d[i, j] = d[i, j] - (left_new[i] * left[j] + right_new[i] * right[j])
        for i in rest:
            d[max(i, p), min(i, p)] = left_new[i]
            d[max(i, q), min(i, q)] = right_new[i]
        d[p, p], d[q, p], d[q, q] = -pp, -qp, -qq
    return entry


def sweep_panel(ref, start, half, base):
    lane = lax.broadcasted_iota(jnp.int32, TILE, 1)
    sub = lax.broadcasted_iota(jnp.int32, TILE, 0)
    rows = [
        [ref[pl.ds(pl.multiple_of(start + 8 * m, 8), 8), 128 * h : 128 * h + 128] for h in range(2)]
        for m in range(4)
    ]
    for m in range(4):
        from_block = lane - (base + 8 * m)
        in_block = (from_block >= 0) & (from_block < 8)
        columns = [[column(rows[g][half], base + 8 * m + j) for j in range(8)] for g in range(4)]
        d = {
            (i, j): jnp.broadcast_to(columns[m][j][i : i + 1, :], TILE)
            for i in range(8)
            for j in range(i + 1)
        }
        entry = invert_block(d)
        new, spread_rows = [], []
        for h in range(2):
            source = -rows[m][h]
            if h == half:
                source = jnp.where(in_block, jnp.where(from_block == sub, 1.0, 0.0), source)
            sources = [jnp.broadcast_to(source[j : j + 1, :], TILE) for j in range(8)]
            spread_rows.append(
                [tree_sum([entry(i, j) * sources[j] for j in range(8)]) for i in range(8)]
            )
            row = spread_rows[h][0]
            for i in range(1, 8):
                row = jnp.where(sub == i, spread_rows[h][i], row)
            new.append(row)
        for g in range(4):
            if g == m:
                continue
            for h in range(2):
                block = rows[g][h]
                if h == half:
                    block = jnp.where(in_block, 0.0, block)
                rows[g][h] = block - tree_sum([columns[g][j] * spread_rows[h][j] for j in range(8)])
        rows[m] = new
    return jnp.concatenate([jnp.concatenate(row, axis=1) for row in rows], axis=0)


def three_parts(x):
    first = x.astype(BF16)
    rest = x - first.astype(F32)
    second = rest.astype(BF16)
    return first, second, (rest - second.astype(F32)).astype(BF16)


def narrow_tn(a, b):
    a1, a2, a3 = three_parts(a)
    b1, b2, b3 = three_parts(b)
    left = jnp.concatenate([a1, a1, a1, a2, a2, a3], axis=0)
    right = jnp.concatenate([b1, b2, b3, b1, b2, b1], axis=0)
    return lax.dot_general(left, right, (((0,), (0,)), ((), ())), preferred_element_type=F32)


def sweep(ref):
    lane = lax.broadcasted_iota(jnp.int32, (256, 256), 1)
    for half in range(2):

        def step(k, carry):
            start = half * 128 + k * 32
            panel = pl.ds(pl.multiple_of(start, 32), 32)
            old = ref[panel, :]
            new = sweep_panel(ref, start, half, k * 32)
            in_panel = (lane >= start) & (lane < start + 32)
            ref[...] = jnp.where(in_panel, 0.0, ref[...]) - narrow_tn(old, new)
            ref[panel, :] = new
            return carry

        lax.fori_loop(0, 4, step, 0)


def dot(a, b):
    return jnp.dot(a, b, precision=HIGH, preferred_element_type=F32)


def dot_tn(a, b):
    return lax.dot_general(a, b, (((0,), (0,)), ((), ())), precision=HIGH, preferred_element_type=F32)


def diagonal_of(gram):
    on_diagonal = lax.broadcasted_iota(jnp.int32, gram.shape, 0) == lax.broadcasted_iota(jnp.int32, gram.shape, 1)
    return jnp.sum(jnp.where(on_diagonal, gram, 0.0), axis=0, keepdims=True)


def diagonal_scale(gram):
    return lax.rsqrt(diagonal_of(gram))


def outer(row):
    rows = jnp.where(lax.broadcasted_iota(jnp.int32, (16, row.shape[1]), 0) == 0, row, 0.0)
    return narrow_tn(rows, rows)


def gram_inverse_kernel(mine_ref, other_ref, out_ref, c_gram_ref):
    c_gram = mine_ref[1] + other_ref[1]
    c_gram_ref[...] = c_gram
    gram = (mine_ref[0] + other_ref[0]) * c_gram
    scale = outer(diagonal_scale(gram))
    out_ref[...] = gram * scale
    sweep(out_ref)
    out_ref[...] = -out_ref[...] * scale


def gram_inverse(mine, other):
    square = jax.ShapeDtypeStruct(mine.shape[1:], F32)
    return pl.pallas_call(
        gram_inverse_kernel,
        out_shape=(square, square),
        in_specs=[WHOLE] * 2,
        out_specs=(WHOLE,) * 2,
        compiler_params=PARAMS,
        cost_estimate=SOLVE_COST,
        name="gram_inverse",
    )(mine, other)


def in_order(mine, other, core):
    first = jnp.where(core == 0, mine, other)
    second = jnp.where(core == 0, other, mine)
    return jnp.concatenate([first[:, None], second[:, None]], axis=1)


def scaled_inverse_kernel(total, core_ref, mine_ref, other_ref, c_ref, inverse_ref, rows_ref):
    size = c_ref.shape[1]
    gram = in_order(mine_ref[...], other_ref[...], core_ref[0]).reshape(size, size)
    squares = diagonal_of(gram)
    scale = jnp.sqrt(squares / total + EPS)
    gram = gram * c_ref[...]
    before = diagonal_scale(gram)
    inverse_ref[...] = gram * outer(before)
    sweep(inverse_ref)
    inverse_ref[...] = -inverse_ref[...]
    rows_ref[...] = jnp.concatenate([before, before * scale, scale] + [scale] * 5, axis=0)


def scaled_inverse(core, mine, other, c_gram, total):
    size = c_gram.shape[1]
    return pl.pallas_call(
        functools.partial(scaled_inverse_kernel, float(total)),
        out_shape=(jax.ShapeDtypeStruct((size, size), F32), jax.ShapeDtypeStruct((8, size), F32)),
        in_specs=[SCALARS] + [WHOLE] * 3,
        out_specs=(WHOLE,) * 2,
        cost_estimate=SOLVE_COST,
        compiler_params=PARAMS,
        name="scaled_inverse",
    )(core, mine, other, c_gram)


def first_product_kernel(core_ref, tensor_ref, mine_ref, other_ref, c_ref, keep_ref, send_ref, held_ref, b_ref, arrived):
    core = core_ref[0]
    points, rows, depth = tensor_ref.shape
    owners, own, rank = keep_ref.shape
    steps = arrived.shape[0]
    height = rows // steps

    def load(i):
        part = pl.ds(pl.multiple_of(i * height, height), height)
        return pltpu.make_async_copy(tensor_ref.at[:, part, :], held_ref.at[:, part, :], arrived.at[i])

    for i in range(steps):
        load(i).start()
    b_ref[...] = in_order(mine_ref[...], other_ref[...], core).reshape(b_ref.shape)
    few = owners // steps
    c_float = c_ref[...].astype(F32)

    def step(i, carry):
        load(i).wait()
        total = None
        for k in range(points):
            block = held_ref[k, pl.ds(pl.multiple_of(i * height, height), height), :]
            term = jnp.dot(block, b_ref[...], preferred_element_type=F32) * c_float[k : k + 1, :]
            total = term if total is None else total + term
        total = total.reshape(few, 2, own, rank)
        keep_ref[pl.ds(i * few, few)] = jnp.where(core == 0, total[:, 0], total[:, 1])
        send_ref[pl.ds(i * few, few)] = jnp.where(core == 0, total[:, 1], total[:, 0])
        return carry

    lax.fori_loop(0, steps, step, 0)


def first_product(core, tensor, mine, other, c_factor, owners):
    points, rows, depth = tensor.shape
    rank = mine.shape[-1]
    part = jax.ShapeDtypeStruct((owners, rows // (2 * owners), rank), F32)
    return pl.pallas_call(
        first_product_kernel,
        out_shape=(part, part),
        in_specs=[SCALARS, pl.BlockSpec(memory_space=pl.ANY)] + [WHOLE] * 3,
        out_specs=(WHOLE,) * 2,
        scratch_shapes=[
            pltpu.VMEM(tensor.shape, BF16),
            pltpu.VMEM((depth, rank), BF16),
            pltpu.SemaphoreType.DMA((4,)),
        ],
        compiler_params=PRODUCT_PARAMS,
        cost_estimate=PRODUCT_COST,
        name="first_product",
    )(core, tensor, mine, other, c_factor)


def second_product_kernel(core_ref, tensor_ref, mine_ref, other_ref, c_ref, keep_ref, send_ref, held_ref, a_ref, sum_ref, column_ref, arrived):
    core = core_ref[0]
    owners, own, rank = keep_ref.shape

    def load(k):
        return pltpu.make_async_copy(tensor_ref.at[k], held_ref.at[k], arrived.at[k])

    for k in range(tensor_ref.shape[0]):
        load(k).start()
    a_rows = in_order(mine_ref[...], other_ref[...], core).reshape(a_ref.shape[1], a_ref.shape[0])
    a_ref[...] = a_rows.T
    sum_ref[...] = jnp.zeros_like(sum_ref)
    points, rank = c_ref.shape
    columns = jnp.concatenate([c_ref[...].astype(F32)] * (8 // points), axis=0).T
    for k in range(points):
        column_ref[k] = jnp.broadcast_to(columns[:, k : k + 1], (rank, 128))

    def step(k, carry):
        load(k).wait()
        term = jnp.dot(a_ref[...], held_ref[k], preferred_element_type=F32)
        sum_ref[...] += term * jnp.concatenate([column_ref[k]] * (term.shape[1] // 128), axis=1)
        return carry

    lax.fori_loop(0, tensor_ref.shape[0], step, 0)
    total = sum_ref[...].T.reshape(owners, 2, own, rank)
    keep_ref[...] = jnp.where(core == 0, total[:, 0], total[:, 1])
    send_ref[...] = jnp.where(core == 0, total[:, 1], total[:, 0])


def second_product(core, tensor, mine, other, c_factor, owners):
    points, depth, rows = tensor.shape
    rank = mine.shape[-1]
    part = jax.ShapeDtypeStruct((owners, rows // (2 * owners), rank), F32)
    return pl.pallas_call(
        second_product_kernel,
        out_shape=(part, part),
        in_specs=[SCALARS, pl.BlockSpec(memory_space=pl.ANY)] + [WHOLE] * 3,
        out_specs=(WHOLE, WHOLE),
        scratch_shapes=[
            pltpu.VMEM(tensor.shape, BF16),
            pltpu.VMEM((rank, depth), BF16),
            pltpu.VMEM((rank, rows), F32),
            pltpu.VMEM((points, rank, 128), F32),
            pltpu.SemaphoreType.DMA((points,)),
        ],
        compiler_params=PRODUCT_PARAMS,
        cost_estimate=PRODUCT_COST,
        name="second_product",
    )(core, tensor, mine, other, c_factor)


def solve_kernel(parts_ref, inverse_ref, raw_ref, rows_ref):
    raw = dot(jnp.sum(parts_ref[...], axis=0), inverse_ref[...])
    raw_ref[...] = raw
    rows_ref[...] = jnp.broadcast_to(raw.astype(BF16)[None], rows_ref.shape)


def solve(parts, inverse, copies):
    own = parts.shape[1:]
    return pl.pallas_call(
        solve_kernel,
        out_shape=(jax.ShapeDtypeStruct(own, F32), jax.ShapeDtypeStruct((copies,) + own, BF16)),
        in_specs=[WHOLE] * 2,
        out_specs=(WHOLE,) * 2,
        compiler_params=PARAMS,
        name="solve",
    )(parts, inverse)


def sum_spread_kernel(parts_ref, out_ref):
    out_ref[...] = jnp.broadcast_to(jnp.sum(parts_ref[...].astype(F32), axis=0)[None], out_ref.shape)


def sum_spread(parts, copies):
    return pl.pallas_call(
        sum_spread_kernel,
        out_shape=jax.ShapeDtypeStruct((copies,) + parts.shape[1:], F32),
        in_specs=[WHOLE],
        out_specs=WHOLE,
        compiler_params=PARAMS,
        name="sum_spread",
    )(parts)


def last_rows_kernel(parts_ref, raw_ref, inverse_ref, rows_ref, a_ref, b_ref):
    a_ref[...] = raw_ref[...] * (1.0 / rows_ref[2:3, :])
    rows = jnp.sum(parts_ref[...], axis=0) * rows_ref[0:1, :]
    b_ref[...] = dot(rows, inverse_ref[...]) * rows_ref[1:2, :]


def last_rows(parts, raw, inverse, rows):
    return pl.pallas_call(
        last_rows_kernel,
        out_shape=(jax.ShapeDtypeStruct(raw.shape, F32), jax.ShapeDtypeStruct(parts.shape[1:], F32)),
        in_specs=[WHOLE] * 4,
        out_specs=(WHOLE,) * 2,
        compiler_params=PARAMS,
        name="last_rows",
    )(parts, raw, inverse, rows)


def gram_strips_kernel(place_ref, rows_ref, keep_ref, send_ref, gram_ref):
    rows = rows_ref[...].reshape(-1, rows_ref.shape[-1])
    gram_ref[...] = lax.dot_general(rows, rows, (((0,), (0,)), ((), ())), preferred_element_type=F32)
    height = keep_ref.shape[0]
    keep_ref[...] = gram_ref[pl.ds(pl.multiple_of(place_ref[1] * height, height), height), :]
    send_ref[...] = gram_ref[pl.ds(pl.multiple_of(place_ref[2] * height, height), height), :]


def gram_strips(place, rows, strips):
    rank = rows.shape[-1]
    return pl.pallas_call(
        gram_strips_kernel,
        out_shape=(jax.ShapeDtypeStruct((rank // strips, rank), F32),) * 2,
        in_specs=[SCALARS, WHOLE],
        out_specs=(WHOLE,) * 2,
        scratch_shapes=[pltpu.VMEM((rank, rank), F32)],
        compiler_params=PARAMS,
        cost_estimate=pl.CostEstimate(flops=10**9, bytes_accessed=10**6, transcendentals=0),
        name="gram_strips",
    )(place, rows)


def pair_spread_kernel(mine_ref, other_ref, out_ref):
    out_ref[...] = jnp.broadcast_to((mine_ref[...] + other_ref[...]).astype(BF16)[None], out_ref.shape)


def pair_spread(mine, other, copies):
    return pl.pallas_call(
        pair_spread_kernel,
        out_shape=jax.ShapeDtypeStruct((copies,) + mine.shape, BF16),
        in_specs=[WHOLE] * 2,
        out_specs=WHOLE,
        compiler_params=PARAMS,
        name="pair_spread",
    )(mine, other)


def rows_grams_kernel(rows_ref, c_ref, gate_ref, out_ref):
    points, rank = c_ref.shape
    rows = rows_ref[...].reshape(-1, rank)
    out_ref[0] = lax.dot_general(rows, rows, (((0,), (0,)), ((), ())), preferred_element_type=F32)
    own = jnp.concatenate([c_ref[...].astype(F32)] * (16 // points), axis=0)
    own = jnp.where(lax.broadcasted_iota(jnp.int32, own.shape, 0) < points, own, 0.0).astype(BF16)
    out_ref[1] = lax.dot_general(own, own, (((0,), (0,)), ((), ())), preferred_element_type=F32)


def rows_grams(rows, c_factor, gate):
    rank = rows.shape[-1]
    return pl.pallas_call(
        rows_grams_kernel,
        out_shape=jax.ShapeDtypeStruct((2, rank, rank), F32),
        in_specs=[WHOLE, WHOLE, pl.BlockSpec(memory_space=pl.ANY)],
        out_specs=WHOLE,
        compiler_params=PARAMS,
        name="rows_grams",
    )(rows, c_factor, gate)


def add_after_kernel(keep_ref, received_ref, gate_ref, out_ref):
    out_ref[...] = keep_ref[...] + received_ref[...]


def add_after(keep, received, gate):
    return pl.pallas_call(
        add_after_kernel,
        out_shape=jax.ShapeDtypeStruct(keep.shape, F32),
        in_specs=[WHOLE, WHOLE, pl.BlockSpec(memory_space=pl.ANY)],
        out_specs=WHOLE,
        compiler_params=PARAMS,
        name="add_after",
    )(keep, received, gate)


def exchange(block, axes):
    return lax.all_to_all(block, axes, 0, 0, tiled=True)


def spread(block, axes):
    return exchange(jnp.broadcast_to(block[None], (lax.axis_size(axes),) + block.shape), axes)


def swap(block):
    return lax.ppermute(block, "op", [(0, 1), (1, 0)])


def shards(tensor, b_start, c_factor):
    points, freq_count, pair_count = tensor.shape
    rank = b_start.shape[1]
    freqs, senses = lax.axis_size("freq"), lax.axis_size("sens")
    core_id = lax.axis_index("op")
    strip = lax.axis_index("sens") * 2
    place = jnp.stack([core_id, strip + core_id, strip + 1 - core_id]).astype(jnp.int32)

    b_mine = spread(b_start, "freq")
    b_other = swap(b_mine)
    b_half = spread(b_mine.reshape(-1, rank), "sens")
    keep, send = first_product(place, tensor, b_mine, b_other, c_factor, senses)
    owned = keep + swap(send)
    grams = rows_grams(b_half, c_factor, owned)
    inverse_one, c_gram = gram_inverse(grams, swap(grams))
    a_raw, a_spread = solve(exchange(owned, "sens"), inverse_one, senses)

    a_mine = exchange(a_spread, "sens")
    strip_keep, strip_send = gram_strips(place, a_mine, 2 * senses)
    strips = exchange(pair_spread(strip_keep, swap(strip_send), freqs), "freq")
    a_other = swap(a_mine)
    keep, send = second_product(place, tensor, a_mine, a_other, c_factor, freqs)
    strips_mine = exchange(sum_spread(strips, senses), "sens")
    strips_other = swap(strips_mine)
    second = exchange(add_after(keep, swap(send), strips_mine), "freq")
    inverse_two, rows = scaled_inverse(place, strips_mine, strips_other, c_gram, freq_count * freqs)
    return last_rows(second, a_raw, inverse_two, rows)


def solution(mesh):
    in_specs = (P("op", "freq", "sens"), P(("sens", "freq", "op"), None), P("op", None))
    out_specs = (P(("freq", "sens", "op"), None), P(("sens", "freq", "op"), None))
    return jax.shard_map(shards, mesh=mesh, in_specs=in_specs, out_specs=out_specs, check_vma=False)
```

```python
import functools

import jax
import jax.numpy as jnp
from jax import lax
from jax.experimental import pallas as pl
from jax.experimental.pallas import tpu as pltpu
from jax.sharding import PartitionSpec as P

EPS = 1e-06
F32 = jnp.float32
BF16 = jnp.bfloat16
HIGH = lax.Precision.HIGHEST
WHOLE = pl.BlockSpec(memory_space=pltpu.VMEM)
TILE = (8, 128)
PRODUCT_PARAMS = pltpu.CompilerParams(vmem_limit_bytes=51 * 2**20)
PARAMS = pltpu.CompilerParams(vmem_limit_bytes=24 * 2**20)
SCALARS = pl.BlockSpec(memory_space=pltpu.SMEM)
PRODUCT_COST = pl.CostEstimate(flops=2 * 10**9, bytes_accessed=6 * 10**6, transcendentals=0)
SOLVE_COST = pl.CostEstimate(flops=2 * 10**10, bytes_accessed=10**6, transcendentals=0)


def tree_sum(terms):
    while len(terms) > 1:
        pairs = [terms[i] + terms[i + 1] for i in range(0, len(terms) - 1, 2)]
        terms = pairs + terms[len(terms) - len(terms) % 2 :]
    return terms[0]


def column(block, lane):
    return jnp.take_along_axis(block, jnp.full(TILE, lane, jnp.int32), axis=1)


def invert_block(d):
    def entry(i, j):
        return d[max(i, j), min(i, j)]

    for p in range(0, 8, 2):
        q = p + 1
        first, cross, second = d[p, p], d[q, p], d[q, q]
        determinant = first * second - cross * cross
        guess = pl.reciprocal(determinant, approx=True)
        guess = guess * (2.0 - determinant * guess)
        rest = [i for i in range(8) if i not in (p, q)]
        left = {i: entry(i, p) for i in rest}
        right = {i: entry(i, q) for i in rest}
        left_new = {i: left[i] * second - right[i] * cross for i in rest}
        right_new = {i: right[i] * first - left[i] * cross for i in rest}
        for i in rest:
            for j in rest:
                if j <= i:
                    d[i, j] = d[i, j] - (left_new[i] * left[j] + right_new[i] * right[j]) * guess
        for i in rest:
            d[max(i, p), min(i, p)] = left_new[i] * guess
            d[max(i, q), min(i, q)] = right_new[i] * guess
        d[p, p], d[q, p], d[q, q] = -(second * guess), cross * guess, -(first * guess)
    return entry


def sweep_panel(ref, start, half, base):
    lane = lax.broadcasted_iota(jnp.int32, TILE, 1)
    sub = lax.broadcasted_iota(jnp.int32, TILE, 0)
    rows = [
        [ref[pl.ds(pl.multiple_of(start + 8 * m, 8), 8), 128 * h : 128 * h + 128] for h in range(2)]
        for m in range(4)
    ]
    for m in range(4):
        from_block = lane - (base + 8 * m)
        in_block = (from_block >= 0) & (from_block < 8)
        columns = [[column(rows[g][half], base + 8 * m + j) for j in range(8)] for g in range(4)]
        d = {
            (i, j): jnp.broadcast_to(columns[m][j][i : i + 1, :], TILE)
            for i in range(8)
            for j in range(i + 1)
        }
        entry = invert_block(d)
        new, spread_rows = [], []
        for h in range(2):
            source = -rows[m][h]
            if h == half:
                source = jnp.where(in_block, jnp.where(from_block == sub, 1.0, 0.0), source)
            sources = [jnp.broadcast_to(source[j : j + 1, :], TILE) for j in range(8)]
            spread_rows.append(
                [tree_sum([entry(i, j) * sources[j] for j in range(8)]) for i in range(8)]
            )
            row = spread_rows[h][0]
            for i in range(1, 8):
                row = jnp.where(sub == i, spread_rows[h][i], row)
            new.append(row)
        for g in range(4):
            if g == m:
                continue
            for h in range(2):
                block = rows[g][h]
                if h == half:
                    block = jnp.where(in_block, 0.0, block)
                rows[g][h] = block - tree_sum([columns[g][j] * spread_rows[h][j] for j in range(8)])
        rows[m] = new
    return jnp.concatenate([jnp.concatenate(row, axis=1) for row in rows], axis=0)


def three_parts(x):
    first = x.astype(BF16)
    rest = x - first.astype(F32)
    second = rest.astype(BF16)
    return first, second, (rest - second.astype(F32)).astype(BF16)


def narrow_tn(a, b):
    a1, a2, a3 = three_parts(a)
    b1, b2, b3 = three_parts(b)
    left = jnp.concatenate([a1, a1, a1, a2, a2, a3], axis=0)
    right = jnp.concatenate([b1, b2, b3, b1, b2, b1], axis=0)
    return lax.dot_general(left, right, (((0,), (0,)), ((), ())), preferred_element_type=F32)


def sweep(ref):
    lane = lax.broadcasted_iota(jnp.int32, (256, 256), 1)
    for half in range(2):

        def step(k, carry):
            start = half * 128 + k * 32
            panel = pl.ds(pl.multiple_of(start, 32), 32)
            old = ref[panel, :]
            new = sweep_panel(ref, start, half, k * 32)
            in_panel = (lane >= start) & (lane < start + 32)
            ref[...] = jnp.where(in_panel, 0.0, ref[...]) - narrow_tn(old, new)
            ref[panel, :] = new
            return carry

        lax.fori_loop(0, 4, step, 0)


def dot(a, b):
    return jnp.dot(a, b, precision=HIGH, preferred_element_type=F32)


def dot_tn(a, b):
    return lax.dot_general(a, b, (((0,), (0,)), ((), ())), precision=HIGH, preferred_element_type=F32)


def diagonal_of(gram):
    on_diagonal = lax.broadcasted_iota(jnp.int32, gram.shape, 0) == lax.broadcasted_iota(jnp.int32, gram.shape, 1)
    return jnp.sum(jnp.where(on_diagonal, gram, 0.0), axis=0, keepdims=True)


def diagonal_scale(gram):
    return lax.rsqrt(diagonal_of(gram))


def outer(row):
    rows = jnp.where(lax.broadcasted_iota(jnp.int32, (16, row.shape[1]), 0) == 0, row, 0.0)
    return narrow_tn(rows, rows)


def gram_inverse_kernel(mine_ref, other_ref, out_ref, c_gram_ref):
    c_gram = mine_ref[1] + other_ref[1]
    c_gram_ref[...] = c_gram
    gram = (mine_ref[0] + other_ref[0]) * c_gram
    scale = outer(diagonal_scale(gram))
    out_ref[...] = gram * scale
    sweep(out_ref)
    out_ref[...] = -out_ref[...] * scale


def gram_inverse(mine, other):
    square = jax.ShapeDtypeStruct(mine.shape[1:], F32)
    return pl.pallas_call(
        gram_inverse_kernel,
        out_shape=(square, square),
        in_specs=[WHOLE] * 2,
        out_specs=(WHOLE,) * 2,
        compiler_params=PARAMS,
        cost_estimate=SOLVE_COST,
        name="gram_inverse",
    )(mine, other)


def in_order(mine, other, core):
    first = jnp.where(core == 0, mine, other)
    second = jnp.where(core == 0, other, mine)
    return jnp.concatenate([first[:, None], second[:, None]], axis=1)


def scaled_inverse_kernel(total, core_ref, mine_ref, other_ref, c_ref, inverse_ref, rows_ref):
    size = c_ref.shape[1]
    gram = in_order(mine_ref[...], other_ref[...], core_ref[0]).reshape(size, size)
    squares = diagonal_of(gram)
    scale = jnp.sqrt(squares / total + EPS)
    gram = gram * c_ref[...]
    before = diagonal_scale(gram)
    inverse_ref[...] = gram * outer(before)
    sweep(inverse_ref)
    inverse_ref[...] = -inverse_ref[...]
    rows_ref[...] = jnp.concatenate([before, before * scale, scale] + [scale] * 5, axis=0)


def scaled_inverse(core, mine, other, c_gram, total):
    size = c_gram.shape[1]
    return pl.pallas_call(
        functools.partial(scaled_inverse_kernel, float(total)),
        out_shape=(jax.ShapeDtypeStruct((size, size), F32), jax.ShapeDtypeStruct((8, size), F32)),
        in_specs=[SCALARS] + [WHOLE] * 3,
        out_specs=(WHOLE,) * 2,
        cost_estimate=SOLVE_COST,
        compiler_params=PARAMS,
        name="scaled_inverse",
    )(core, mine, other, c_gram)


def first_product_kernel(core_ref, tensor_ref, mine_ref, other_ref, c_ref, keep_ref, send_ref, held_ref, b_ref, arrived):
    core = core_ref[0]
    points, rows, depth = tensor_ref.shape
    owners, own, rank = keep_ref.shape
    steps = arrived.shape[0]
    height = rows // steps

    def load(i):
        part = pl.ds(pl.multiple_of(i * height, height), height)
        return pltpu.make_async_copy(tensor_ref.at[:, part, :], held_ref.at[:, part, :], arrived.at[i])

    for i in range(steps):
        load(i).start()
    b_ref[...] = in_order(mine_ref[...], other_ref[...], core).reshape(b_ref.shape)
    few = owners // steps
    c_float = c_ref[...].astype(F32)

    def step(i, carry):
        load(i).wait()
        total = None
        for k in range(points):
            block = held_ref[k, pl.ds(pl.multiple_of(i * height, height), height), :]
            term = jnp.dot(block, b_ref[...], preferred_element_type=F32) * c_float[k : k + 1, :]
            total = term if total is None else total + term
        total = total.reshape(few, 2, own, rank)
        keep_ref[pl.ds(i * few, few)] = jnp.where(core == 0, total[:, 0], total[:, 1])
        send_ref[pl.ds(i * few, few)] = jnp.where(core == 0, total[:, 1], total[:, 0])
        return carry

    lax.fori_loop(0, steps, step, 0)


def first_product(core, tensor, mine, other, c_factor, owners):
    points, rows, depth = tensor.shape
    rank = mine.shape[-1]
    part = jax.ShapeDtypeStruct((owners, rows // (2 * owners), rank), F32)
    return pl.pallas_call(
        first_product_kernel,
        out_shape=(part, part),
        in_specs=[SCALARS, pl.BlockSpec(memory_space=pl.ANY)] + [WHOLE] * 3,
        out_specs=(WHOLE,) * 2,
        scratch_shapes=[
            pltpu.VMEM(tensor.shape, BF16),
            pltpu.VMEM((depth, rank), BF16),
            pltpu.SemaphoreType.DMA((4,)),
        ],
        compiler_params=PRODUCT_PARAMS,
        cost_estimate=PRODUCT_COST,
        name="first_product",
    )(core, tensor, mine, other, c_factor)


def second_product_kernel(core_ref, tensor_ref, mine_ref, other_ref, c_ref, keep_ref, send_ref, held_ref, a_ref, sum_ref, column_ref, arrived):
    core = core_ref[0]
    owners, own, rank = keep_ref.shape

    def load(k):
        return pltpu.make_async_copy(tensor_ref.at[k], held_ref.at[k], arrived.at[k])

    for k in range(tensor_ref.shape[0]):
        load(k).start()
    a_rows = in_order(mine_ref[...], other_ref[...], core).reshape(a_ref.shape[1], a_ref.shape[0])
    a_ref[...] = a_rows.T
    sum_ref[...] = jnp.zeros_like(sum_ref)
    points, rank = c_ref.shape
    columns = jnp.concatenate([c_ref[...].astype(F32)] * (8 // points), axis=0).T
    for k in range(points):
        column_ref[k] = jnp.broadcast_to(columns[:, k : k + 1], (rank, 128))

    def step(k, carry):
        load(k).wait()
        term = jnp.dot(a_ref[...], held_ref[k], preferred_element_type=F32)
        sum_ref[...] += term * jnp.concatenate([column_ref[k]] * (term.shape[1] // 128), axis=1)
        return carry

    lax.fori_loop(0, tensor_ref.shape[0], step, 0)
    total = sum_ref[...].T.reshape(owners, 2, own, rank)
    keep_ref[...] = jnp.where(core == 0, total[:, 0], total[:, 1])
    send_ref[...] = jnp.where(core == 0, total[:, 1], total[:, 0])


def second_product(core, tensor, mine, other, c_factor, owners):
    points, depth, rows = tensor.shape
    rank = mine.shape[-1]
    part = jax.ShapeDtypeStruct((owners, rows // (2 * owners), rank), F32)
    return pl.pallas_call(
        second_product_kernel,
        out_shape=(part, part),
        in_specs=[SCALARS, pl.BlockSpec(memory_space=pl.ANY)] + [WHOLE] * 3,
        out_specs=(WHOLE, WHOLE),
        scratch_shapes=[
            pltpu.VMEM(tensor.shape, BF16),
            pltpu.VMEM((rank, depth), BF16),
            pltpu.VMEM((rank, rows), F32),
            pltpu.VMEM((points, rank, 128), F32),
            pltpu.SemaphoreType.DMA((points,)),
        ],
        compiler_params=PRODUCT_PARAMS,
        cost_estimate=PRODUCT_COST,
        name="second_product",
    )(core, tensor, mine, other, c_factor)


def solve_kernel(parts_ref, inverse_ref, raw_ref, rows_ref):
    raw = dot(jnp.sum(parts_ref[...], axis=0), inverse_ref[...])
    raw_ref[...] = raw
    rows_ref[...] = jnp.broadcast_to(raw.astype(BF16)[None], rows_ref.shape)


def solve(parts, inverse, copies):
    own = parts.shape[1:]
    return pl.pallas_call(
        solve_kernel,
        out_shape=(jax.ShapeDtypeStruct(own, F32), jax.ShapeDtypeStruct((copies,) + own, BF16)),
        in_specs=[WHOLE] * 2,
        out_specs=(WHOLE,) * 2,
        compiler_params=PARAMS,
        name="solve",
    )(parts, inverse)


def sum_spread_kernel(parts_ref, out_ref):
    out_ref[...] = jnp.broadcast_to(jnp.sum(parts_ref[...].astype(F32), axis=0)[None], out_ref.shape)


def sum_spread(parts, copies):
    return pl.pallas_call(
        sum_spread_kernel,
        out_shape=jax.ShapeDtypeStruct((copies,) + parts.shape[1:], F32),
        in_specs=[WHOLE],
        out_specs=WHOLE,
        compiler_params=PARAMS,
        name="sum_spread",
    )(parts)


def last_rows_kernel(parts_ref, raw_ref, inverse_ref, rows_ref, a_ref, b_ref):
    a_ref[...] = raw_ref[...] * (1.0 / rows_ref[2:3, :])
    rows = jnp.sum(parts_ref[...].astype(F32), axis=0) * rows_ref[0:1, :]
    b_ref[...] = dot(rows, inverse_ref[...]) * rows_ref[1:2, :]


def last_rows(parts, raw, inverse, rows):
    return pl.pallas_call(
        last_rows_kernel,
        out_shape=(jax.ShapeDtypeStruct(raw.shape, F32), jax.ShapeDtypeStruct(parts.shape[1:], F32)),
        in_specs=[WHOLE] * 4,
        out_specs=(WHOLE,) * 2,
        compiler_params=PARAMS,
        name="last_rows",
    )(parts, raw, inverse, rows)


def gram_strips_kernel(place_ref, rows_ref, keep_ref, send_ref, gram_ref):
    rows = rows_ref[...].reshape(-1, rows_ref.shape[-1])
    gram_ref[...] = lax.dot_general(rows, rows, (((0,), (0,)), ((), ())), preferred_element_type=F32)
    height = keep_ref.shape[0]
    keep_ref[...] = gram_ref[pl.ds(pl.multiple_of(place_ref[1] * height, height), height), :]
    send_ref[...] = gram_ref[pl.ds(pl.multiple_of(place_ref[2] * height, height), height), :]


def gram_strips(place, rows, strips):
    rank = rows.shape[-1]
    return pl.pallas_call(
        gram_strips_kernel,
        out_shape=(jax.ShapeDtypeStruct((rank // strips, rank), F32),) * 2,
        in_specs=[SCALARS, WHOLE],
        out_specs=(WHOLE,) * 2,
        scratch_shapes=[pltpu.VMEM((rank, rank), F32)],
        compiler_params=PARAMS,
        cost_estimate=pl.CostEstimate(flops=10**9, bytes_accessed=10**6, transcendentals=0),
        name="gram_strips",
    )(place, rows)


def pair_spread_kernel(mine_ref, other_ref, out_ref):
    out_ref[...] = jnp.broadcast_to((mine_ref[...] + other_ref[...]).astype(BF16)[None], out_ref.shape)


def pair_spread(mine, other, copies):
    return pl.pallas_call(
        pair_spread_kernel,
        out_shape=jax.ShapeDtypeStruct((copies,) + mine.shape, BF16),
        in_specs=[WHOLE] * 2,
        out_specs=WHOLE,
        compiler_params=PARAMS,
        name="pair_spread",
    )(mine, other)


def rows_grams_kernel(rows_ref, c_ref, gate_ref, out_ref):
    points, rank = c_ref.shape
    rows = rows_ref[...].reshape(-1, rank)
    out_ref[0] = lax.dot_general(rows, rows, (((0,), (0,)), ((), ())), preferred_element_type=F32)
    own = jnp.concatenate([c_ref[...].astype(F32)] * (16 // points), axis=0)
    own = jnp.where(lax.broadcasted_iota(jnp.int32, own.shape, 0) < points, own, 0.0).astype(BF16)
    out_ref[1] = lax.dot_general(own, own, (((0,), (0,)), ((), ())), preferred_element_type=F32)


def rows_grams(rows, c_factor, gate):
    rank = rows.shape[-1]
    return pl.pallas_call(
        rows_grams_kernel,
        out_shape=jax.ShapeDtypeStruct((2, rank, rank), F32),
        in_specs=[WHOLE, WHOLE, pl.BlockSpec(memory_space=pl.ANY)],
        out_specs=WHOLE,
        compiler_params=PARAMS,
        name="rows_grams",
    )(rows, c_factor, gate)


def add_after_kernel(keep_ref, received_ref, gate_ref, out_ref):
    out_ref[...] = (keep_ref[...] + received_ref[...]).astype(BF16)


def add_after(keep, received, gate):
    return pl.pallas_call(
        add_after_kernel,
        out_shape=jax.ShapeDtypeStruct(keep.shape, BF16),
        in_specs=[WHOLE, WHOLE, pl.BlockSpec(memory_space=pl.ANY)],
        out_specs=WHOLE,
        compiler_params=PARAMS,
        name="add_after",
    )(keep, received, gate)


def exchange(block, axes):
    return lax.all_to_all(block, axes, 0, 0, tiled=True)


def spread(block, axes):
    return exchange(jnp.broadcast_to(block[None], (lax.axis_size(axes),) + block.shape), axes)


def swap(block):
    return lax.ppermute(block, "op", [(0, 1), (1, 0)])


def shards(tensor, b_start, c_factor):
    points, freq_count, pair_count = tensor.shape
    rank = b_start.shape[1]
    freqs, senses = lax.axis_size("freq"), lax.axis_size("sens")
    core_id = lax.axis_index("op")
    strip = lax.axis_index("sens") * 2
    place = jnp.stack([core_id, strip + core_id, strip + 1 - core_id]).astype(jnp.int32)

    b_mine = spread(b_start, "freq")
    b_other = swap(b_mine)
    b_half = spread(b_mine.reshape(-1, rank), "sens")
    keep, send = first_product(place, tensor, b_mine, b_other, c_factor, senses)
    owned = keep + swap(send)
    grams = rows_grams(b_half, c_factor, owned)
    inverse_one, c_gram = gram_inverse(grams, swap(grams))
    a_raw, a_spread = solve(exchange(owned, "sens"), inverse_one, senses)

    a_mine = exchange(a_spread, "sens")
    strip_keep, strip_send = gram_strips(place, a_mine, 2 * senses)
    strips = exchange(pair_spread(strip_keep, swap(strip_send), freqs), "freq")
    a_other = swap(a_mine)
    keep, send = second_product(place, tensor, a_mine, a_other, c_factor, freqs)
    strips_mine = exchange(sum_spread(strips, senses), "sens")
    strips_other = swap(strips_mine)
    second = exchange(add_after(keep, swap(send), strips_mine), "freq")
    inverse_two, rows = scaled_inverse(place, strips_mine, strips_other, c_gram, freq_count * freqs)
    return last_rows(second, a_raw, inverse_two, rows)


def solution(mesh):
    in_specs = (P("op", "freq", "sens"), P(("sens", "freq", "op"), None), P("op", None))
    out_specs = (P(("freq", "sens", "op"), None), P(("sens", "freq", "op"), None))
    return jax.shard_map(shards, mesh=mesh, in_specs=in_specs, out_specs=out_specs, check_vma=False)
```
